128 devices in a mesh: blk: 32 (over y_lo, x, z), cent: 4 (over y_hi, core).
Axes of the slice: x: 4, y: 4 (y_hi: 2, y_lo: 2; y = y_hi * 2 + y_lo), z: 4, core: 2. Of those that a mesh axis runs over, the one named last changes fastest.
Arguments:
- descriptors: bfloat16 [24576, 1024], P('blk'), may hold values from -6 to 6
- landmarks: bfloat16 [4096, 1024], P('blk'), may hold values from -6 to 6
- whitening: bfloat16 [4096, 4096], P('blk', 'cent'), may hold values from -0.09375 to 0.09375
- centroids: bfloat16 [4096, 4096], P('cent'), may hold values from -8 to 8, as said below
Outputs:
- assign: bfloat16 [24576, 4096], P('blk', 'cent')
- new_centroids: float32 [4096, 4096], P('blk', 'cent')
The draws below stay inside these ranges and needn't reach their ends.
Inputs may be any that keep to these rules, and one draw needn't show every extreme that they name: `centroids`: centroid coordinates.
All inputs are finite; a program needn't handle non-finite values.
Results may differ from the reference program's by a relative error of at most 0.03.
Values may be sent and summed in bfloat16 or wider, within the bound.
A program may use at most 128 MiB of HBM per device.

```python
import math
import jax
import jax.numpy as jnp
from jax import lax

D = 1024
M = 4096
R = 4096
C = 4096
N = 24576


def draw_centroids(key, part):
    base = jax.random.normal(key, (C, R), jnp.float32) * R ** (-0.5)
    return jnp.clip(base, -8.0, 8.0).astype(jnp.bfloat16)


def block_levels(own_key, extent, shards, low, top_value):
    factor_of, own = 1.0, jax.random.fold_in(own_key, 6)
    for dim, blocks in shards:
        draws = jnp.exp(jax.random.uniform(jax.random.fold_in(own, dim), (blocks,), jnp.float32, low / len(shards), top_value / len(shards)))
        factor_of = factor_of * jnp.repeat(draws, extent[dim] // blocks).reshape([-1 if axis == dim else 1 for axis in range(len(extent))])
    return factor_of


def centred(stream_key, extent, width, reach, split=(), dtype=jnp.bfloat16):
    drawn = width * jax.random.normal(stream_key, extent, jnp.float32)
    if split:
        drawn = drawn * block_levels(stream_key, extent, split, -0.22, 0.18)
    return jnp.clip(drawn, -reach, reach).astype(dtype)


def setup_inputs(seed: int = 0) -> dict:
    arg_keys = jax.random.split(jax.random.key(seed), 5)
    return {
        "descriptors": centred(arg_keys[0], (N, D), 1.0, 6.0, ((0, 32),)),
        "landmarks": centred(arg_keys[1], (M, D), 1.0, 6.0, ((0, 32),)),
        "whitening": centred(arg_keys[2], (M, R), M ** -0.5, 0.09375, ((0, 32), (1, 4))),
        "centroids": draw_centroids(jax.random.fold_in(arg_keys[4], 71), 0),
    }


def unit_rows(values):
    wide = values.astype(jnp.float32)
    sum_sq = lax.optimization_barrier(jnp.sum(wide * wide, axis=1, keepdims=True))
    scale = lax.rsqrt(sum_sq + 1e-06)
    return (wide * scale).astype(jnp.bfloat16)

def reference(descriptors, landmarks, whitening, centroids):
    unit_desc = unit_rows(descriptors)
    unit_land = unit_rows(landmarks)
    sharpness = math.sqrt(D)
    cosine = jnp.dot(unit_desc, unit_land.T, preferred_element_type=jnp.float32)
    kernel = jnp.exp(sharpness * cosine).astype(jnp.bfloat16)
    features = jnp.dot(kernel, whitening, preferred_element_type=jnp.float32).astype(jnp.bfloat16)
    logits = jnp.dot(features, centroids.T, preferred_element_type=jnp.float32)
    row_top = lax.optimization_barrier(jnp.max(logits, axis=1, keepdims=True))
    weights = jnp.exp(logits - row_top)
    row_total = lax.optimization_barrier(jnp.sum(weights, axis=1, keepdims=True))
    assign = (weights / row_total).astype(jnp.bfloat16)
    counts = lax.optimization_barrier(jnp.sum(assign.astype(jnp.float32), axis=0))
    sums = jnp.dot(features.T, assign, preferred_element_type=jnp.float32)
    return (assign, sums / jnp.maximum(counts, 1.0)[None, :])
```

```python
import math

import jax
import jax.numpy as jnp
from jax import lax
from jax.experimental import pallas as pl
from jax.experimental.pallas import tpu as pltpu
from jax.sharding import PartitionSpec as P

MESH = pl.DeviceIdType.MESH
F32 = jnp.float32
BF16 = jnp.bfloat16

ROWS = 768
DEPTH = 1024
BLOCK = 128
GROUP = 4 * BLOCK
LAND = 8 * GROUP
HALF = 512
COLS = 1024
NSEM = 96


def dot(a, b, ca, cb):
    return lax.dot_general(a, b, (((ca,), (cb,)), ((), ())), preferred_element_type=F32)


def normalized(values):
    wide = values.astype(F32)
    sum_sq = jnp.sum(wide * wide, axis=1, keepdims=True)
    return (wide * lax.rsqrt(sum_sq + 1e-06)).astype(BF16)


def body(
    desc_hbm, land_hbm, white_hbm, cent_hbm, assign_hbm, out_hbm,
    desc, seed, land, white, kern, feat, cent, logit, assign_t,
    recv1, part1, recv2, part2, recv3, stat, count, out_v,
    send_sem, recv_sem, local_sem,
):
    blk, col = lax.axis_index("blk"), lax.axis_index("cent")
    y_lo, x, z = blk // 16, (blk // 4) % 4, blk % 4
    y_hi, core = col // 2, col % 2
    y = y_hi * 2 + y_lo
    away = (y_lo + core) % 2
    is_away, is_home = away == 1, away == 0

    def device(xx, yy, zz, cc):
        xx, yy, zz, cc = xx % 4, yy % 4, zz % 4, cc % 2
        return {"blk": (yy % 2) * 16 + xx * 4 + zz, "cent": (yy // 2) * 2 + cc}

    def on_a(d):
        return device(x + (1 - core) * (d + 4), y, z + core * (d + 4), core)

    def on_b(d):
        return device(x + core * (d + 4), y, z + (1 - core) * (d + 4), core)

    pa = x * (1 - core) + z * core
    pb = z * (1 - core) + x * core
    sibling = device(x, y, z, core + 1)
    swap_y = y + 1 - 2 * y_lo
    swap = device(x, swap_y, z, core + 1)
    other = device(x, 7 - y, z, core + 1)
    y_up, y_down = device(x, y + 1, z, core), device(x, y + 3, z, core)
    y_far, y_far_sib = device(x, y + 2, z, core), device(x, y + 2, z, core + 1)
    y_pair = device(x, swap_y, z, core)

    started = []
    counter = [0]

    def copy(src, dst, target, cond=None):
        k = counter[0]
        counter[0] += 1
        c = pltpu.make_async_remote_copy(
            src_ref=src, dst_ref=dst, send_sem=send_sem.at[k], recv_sem=recv_sem.at[k],
            device_id=target, device_id_type=MESH,
        )
        started.append((c, cond))
        return c

    def when(cond, f):
        pl.when(cond)(f)

    load_seed = pltpu.make_async_copy(land_hbm, seed, local_sem.at[0])
    load_desc = pltpu.make_async_copy(desc_hbm, desc.at[0], local_sem.at[1])
    load_seed.start()
    load_desc.start()
    load_cent = [
        pltpu.make_async_copy(cent_hbm.at[:, pl.ds(p * HALF, HALF)], cent.at[p], local_sem.at[2 + p])
        for p in range(8)
    ]
    load_white = [
        pltpu.make_async_copy(
            white_hbm.at[:, pl.ds(h * HALF, HALF)], white.at[h, pl.ds(0, BLOCK)], local_sem.at[10 + h]
        )
        for h in range(2)
    ]

    barrier = pltpu.get_barrier_semaphore()
    partners = [
        sibling, on_a(1), on_a(-1), on_a(2), on_b(1), on_b(-1), on_b(2),
        y_up, y_down, y_far, y_far_sib, swap, other,
    ]
    for target in partners:
        pl.semaphore_signal(barrier, inc=1, device_id=target, device_id_type=MESH)

    when(is_home, lambda: [c.start() for c in load_white] and None)
    load_seed.wait()
    seed[...] = normalized(seed[...])

    @pl.when(is_home)
    def _():
        land[pl.ds(0, BLOCK), :] = seed[...]

    pl.semaphore_wait(barrier, len(partners))

    swap_land = copy(seed, land.at[pl.ds(0, BLOCK)], swap, is_away)
    swap_white = [
        copy(white_hbm.at[:, pl.ds(h * HALF, HALF)], white.at[h, pl.ds(0, BLOCK)], swap, is_away)
        for h in range(2)
    ]
    CUT = 256
    swap_desc = [
        copy(desc.at[0, pl.ds(0, CUT)], desc.at[1, pl.ds(0, CUT)], swap, is_away),
        copy(desc.at[0, pl.ds(CUT, ROWS - CUT)], desc.at[1, pl.ds(CUT, ROWS - CUT)], other, is_away),
    ]

    class Ring:
        def __init__(self, at, size, to):
            def go(src, dst, rows, half, d):
                lo = half * (rows // 2)
                n = rows if half == 0 and dst != 2 else rows // 2
                return copy(at(src, lo, n), at(dst, lo, n), to(d))

            self.up = go(0, 3, size, 0, 1)
            self.down = go(0, 1, size, 0, -1)
            self.fwd_up = go(3, 2, size, 0, 1)
            self.fwd_down = go(1, 2, size, 1, -1)

    def land_a(slot, lo, n):
        return land.at[pl.ds(slot * BLOCK + lo, n)]

    def land_b(slot, lo, n):
        return land.at[pl.ds(slot * GROUP + lo, n)]

    def white_a(h):
        return lambda slot, lo, n: white.at[h, pl.ds(slot * BLOCK + lo, n)]

    def white_b(h):
        return lambda slot, lo, n: white.at[h, pl.ds(slot * GROUP + lo, n)]

    la = Ring(land_a, BLOCK, on_a)
    wa = [Ring(white_a(h), BLOCK, on_a) for h in range(2)]
    lb = Ring(land_b, GROUP, on_b)
    wb = [Ring(white_b(h), GROUP, on_b) for h in range(2)]

    def to_sibling(at, slot):
        return copy(at(slot, 0, GROUP), at(4 + slot, 0, GROUP), sibling)

    ls = [to_sibling(land_b, s) for s in range(4)]
    ws = [[to_sibling(white_b(h), s) for s in range(4)] for h in range(2)]

    @pl.when(is_home)
    def _():
        la.up.start()
        la.down.start()
        for h in range(2):
            load_white[h].wait()
            wa[h].up.start()
            wa[h].down.start()

    @pl.when(is_away)
    def _():
        swap_land.start()
        for h in range(2):
            swap_white[h].start()

    load_desc.wait()

    @pl.loop(0, 3)
    def _(i):
        s = pl.ds(pl.multiple_of(i * 256, 256), 256)
        desc[0, s, :] = normalized(desc[0, s, :])

    @pl.when(is_away)
    def _():
        swap_desc[0].start()
        swap_desc[1].start()
        swap_land.wait_recv()
        la.up.start()
        la.down.start()
        for h in range(2):
            swap_white[h].wait_recv()
            wa[h].up.start()
            wa[h].down.start()

    def forward(ring):
        ring.up.wait_recv()
        ring.fwd_up.start()
        ring.down.wait_recv()
        ring.fwd_down.start()

    def finish(ring):
        ring.fwd_up.wait_recv()
        ring.fwd_down.wait_recv()

    def stage2(ring, sib):
        ring.up.start()
        ring.down.start()
        sib[0].start()

    def stage2_forward(ring, sib):
        forward(ring)
        sib[3].start()
        sib[1].start()

    for c in load_cent:
        c.start()

    sharpness = math.sqrt(DEPTH)

    def kernel_group(g):
        cols = pl.ds(g * GROUP, GROUP)
        cosine = dot(desc[away], land[cols, :], 1, 1)
        kern[:, cols] = jnp.exp(sharpness * cosine).astype(BF16)

    forward(la)
    finish(la)
    stage2(lb, ls)
    forward(wa[0])
    forward(wa[1])

    @pl.when(is_away)
    def _():
        swap_desc[0].wait_recv()
        swap_desc[1].wait_recv()

    kernel_group(0)
    ls[0].wait_recv()
    kernel_group(4)
    finish(wa[0])
    finish(wa[1])
    stage2_forward(lb, ls)
    stage2(wb[0], ws[0])
    kernel_group(3)
    kernel_group(1)
    ls[3].wait_recv()
    kernel_group(7)
    ls[1].wait_recv()
    kernel_group(5)
    finish(lb)
    ls[2].start()
    kernel_group(2)
    stage2_forward(wb[0], ws[0])
    stage2(wb[1], ws[1])
    ls[2].wait_recv()
    kernel_group(6)
    finish(wb[0])
    ws[0][2].start()

    def features(h):
        for s in range(4):
            ws[h][s].wait_recv()
        slot = (1 - away) * (y * 2 + h) + away * (8 + h)

        @pl.loop(0, 3)
        def _(i):
            s = pl.ds(pl.multiple_of(i * 256, 256), 256)
            feat[slot, s, :] = dot(kern[s, :], white[h], 1, 0).astype(BF16)

    own = [y * 2 + h for h in range(2)]
    f_far = [copy(feat.at[own[h]], feat.at[own[h]], y_far, is_home) for h in range(2)]
    f_up = [copy(feat.at[8 + h], feat.at[own[h]], y_up, is_away) for h in range(2)]
    f_down = [copy(feat.at[8 + h], feat.at[own[h]], y_down, is_away) for h in range(2)]

    def slot_of(r, h):
        return ((y + r) % 4) * 2 + h

    f_sib = [
        [copy(feat.at[slot_of(r, h)], feat.at[slot_of(r, h)], sibling, is_home) for r in range(4)]
        for h in range(2)
    ]

    def send_features(h):
        @pl.when(is_home)
        def _():
            f_far[h].start()
            f_sib[h][0].start()

        @pl.when(is_away)
        def _():
            f_up[h].start()
            f_down[h].start()

    features(0)
    send_features(0)
    stage2_forward(wb[1], ws[1])
    finish(wb[1])
    ws[1][2].start()
    features(1)
    send_features(1)

    for c in load_cent:
        c.wait()
    arrived = {1: f_down, 3: f_up, 2: f_far}
    for h in range(2):
        for r in (0, 1, 3, 2):
            if r == 0:
                when(is_away, lambda h=h: f_sib[h][0].wait_recv())
            else:

                @pl.when(is_home)
                def _(h=h, r=r):
                    arrived[r][h].wait_recv()
                    f_sib[h][r].start()

                when(is_away, lambda h=h, r=r: f_sib[h][r].wait_recv())
            slot = slot_of(r, h)
            update = dot(cent[slot], feat[slot], 1, 1)
            if h == 0 and r == 0:
                logit[...] = update
            else:
                logit[...] += update

    top = jnp.max(logit[...], axis=0, keepdims=True)
    weights = jnp.exp(logit[...] - top)
    logit[...] = weights
    total = jnp.sum(weights, axis=0, keepdims=True)
    stat[0, 0:1, :] = top
    stat[0, 1:2, :] = total
    stat_copies = [
        copy(stat.at[0], stat.at[i + 1], target)
        for i, target in enumerate((sibling, y_far, y_far_sib))
    ]
    for c in stat_copies:
        c.start()
    for c in stat_copies:
        c.wait_recv()
    tops = [stat[i, 0:1, :] for i in range(4)]
    all_top = jnp.maximum(jnp.maximum(tops[0], tops[1]), jnp.maximum(tops[2], tops[3]))
    all_total = sum(stat[i, 1:2, :] * jnp.exp(tops[i] - all_top) for i in range(4))
    factor = jnp.exp(tops[0] - all_top) / all_total
    assign_t[...] = (logit[...] * factor).astype(BF16)

    def partial_sum(ta, yy):
        ta = ta % 4
        parts = []
        for b in range(4):
            xb = (1 - core) * ta + core * b
            zb = (1 - core) * b + core * ta
            lanes = pl.ds(pl.multiple_of(zb * 128, 128), 128)
            parts.append(feat[yy * 4 + xb, :, lanes])
        return dot(assign_t[...], jnp.concatenate(parts, axis=1), 1, 0)

    X0, X1, Y0, Y1, Z0, Z1 = range(6)
    rs1 = [
        copy(cent.at[0], recv1.at[X0], on_a(1)),
        copy(cent.at[1], recv1.at[X1], on_a(-1)),
        copy(cent.at[2], recv1.at[Y1], on_a(1)),
        copy(cent.at[3], recv1.at[Y0], on_a(-1)),
        copy(cent.at[4], recv1.at[Z0], on_a(1)),
        copy(cent.at[5], recv1.at[Z1], on_a(-1)),
    ]
    cent[0] = partial_sum(pa + 2, 0).astype(BF16)
    rs1[0].start()
    cent[1] = partial_sum(pa + 2, 1).astype(BF16)
    rs1[1].start()
    cent[2] = partial_sum(pa + 1, 1).astype(BF16)
    rs1[2].start()
    cent[3] = partial_sum(pa + 3, 0).astype(BF16)
    rs1[3].start()

    ones = jnp.ones((8, ROWS), BF16)
    count[0] = dot(ones, assign_t[...], 1, 1)
    count_a = [copy(count.at[0], count.at[1 + i], on_a(d)) for i, d in enumerate((1, -1, 2))]
    count_b = [copy(count.at[4], count.at[5 + i], on_b(d)) for i, d in enumerate((1, -1, 2))]
    count_y = copy(count.at[8], count.at[9], y_pair)
    for c in count_a:
        c.start()

    cent[4] = partial_sum(pa + 1, 0).astype(BF16)
    cent[5] = partial_sum(pa + 3, 1).astype(BF16)
    cent[6] = partial_sum(pa, 0).astype(BF16)
    cent[7] = partial_sum(pa, 1).astype(BF16)

    @pl.when(is_away)
    def _():
        swap_desc[0].wait_send()
        swap_desc[1].wait_send()

    @pl.loop(0, 6)
    def _(i):
        s = pl.ds(pl.multiple_of(i * 128, 128), 128)
        desc[0, s, :] = assign_t[:, s].T

    store_assign = pltpu.make_async_copy(desc.at[0], assign_hbm, local_sem.at[12])
    store_assign.start()

    for c in count_a:
        c.wait_recv()
    count[4] = count[0] + count[1] + count[2] + count[3]
    for c in count_b:
        c.start()

    rs1[0].wait_recv()
    cent[4] = (cent[4].astype(F32) + recv1[X0].astype(F32)).astype(BF16)
    rs1[4].start()
    rs1[1].wait_recv()
    cent[5] = (cent[5].astype(F32) + recv1[X1].astype(F32)).astype(BF16)
    rs1[5].start()

    for c in count_b:
        c.wait_recv()
    count[8] = count[4] + count[5] + count[6] + count[7]
    count_y.start()

    rs1[2].wait_recv()
    rs1[3].wait_recv()
    up, down, far = (pb + 1) % 4, (pb + 3) % 4, (pb + 2) % 4
    rs1[4].wait_recv()
    for b in range(4):
        s = pl.ds(b * 128, 128)
        total = cent[6, :, s].astype(F32) + recv1[Y0, :, s].astype(F32) + recv1[Z0, :, s].astype(F32)
        part1[b] = total.astype(BF16)
    rs1[5].wait_recv()
    for b in range(4):
        s = pl.ds(b * 128, 128)
        total = cent[7, :, s].astype(F32) + recv1[Y1, :, s].astype(F32) + recv1[Z1, :, s].astype(F32)
        part1[4 + b] = total.astype(BF16)

    rs2 = [
        copy(part1.at[far], recv2.at[X0], on_b(1)),
        copy(part1.at[4 + far], recv2.at[X1], on_b(-1)),
        copy(part1.at[4 + up], recv2.at[Y1], on_b(1)),
        copy(part1.at[down], recv2.at[Y0], on_b(-1)),
        copy(part2.at[0], recv2.at[Z0], on_b(1)),
        copy(part2.at[1], recv2.at[Z1], on_b(-1)),
    ]
    for c in rs2[:4]:
        c.start()
    rs2[0].wait_recv()
    part2[0] = (part1[up].astype(F32) + recv2[X0].astype(F32)).astype(BF16)
    rs2[4].start()
    rs2[1].wait_recv()
    part2[1] = (part1[4 + down].astype(F32) + recv2[X1].astype(F32)).astype(BF16)
    rs2[5].start()
    for c in rs2[2:]:
        c.wait_recv()

    part2[2] = (part1[pb].astype(F32) + recv2[Y0].astype(F32) + recv2[Z0].astype(F32)).astype(BF16)
    part2[3] = (part1[4 + pb].astype(F32) + recv2[Y1].astype(F32) + recv2[Z1].astype(F32)).astype(BF16)
    rs3 = copy(part2.at[3 - y_lo], recv3, y_pair)
    rs3.start()
    count_y.wait_recv()
    counts = count[8, 0:1, :] + count[9, 0:1, :]
    rs3.wait_recv()
    sums = part2[2 + y_lo].astype(F32) + recv3[...].astype(F32)
    out_v[...] = sums.T / jnp.maximum(counts, 1.0)
    store_out = pltpu.make_async_copy(out_v, out_hbm, local_sem.at[13])
    store_out.start()

    for c, cond in started:
        if any(c is d for d in swap_desc):
            continue
        if cond is None:
            c.wait_send()
        else:
            when(cond, lambda c=c: c.wait_send())
    store_assign.wait()
    store_out.wait()


def per_device(descriptors, landmarks, whitening, centroids):
    vmem = pltpu.VMEM
    hbm = pl.BlockSpec(memory_space=pl.ANY)
    flops = 2 * ROWS * LAND * DEPTH * 4
    return pl.pallas_call(
        body,
        out_shape=(
            jax.ShapeDtypeStruct((ROWS, COLS), BF16),
            jax.ShapeDtypeStruct((BLOCK, COLS), F32),
        ),
        in_specs=[hbm] * 4,
        out_specs=(hbm, hbm),
        scratch_shapes=[
            vmem((2, ROWS, DEPTH), BF16),
            vmem((BLOCK, DEPTH), BF16),
            vmem((LAND, DEPTH), BF16),
            vmem((2, LAND, HALF), BF16),
            vmem((ROWS, LAND), BF16),
            vmem((10, ROWS, HALF), BF16),
            vmem((8, COLS, HALF), BF16),
            vmem((COLS, ROWS), F32),
            vmem((COLS, ROWS), BF16),
            vmem((6, COLS, HALF), BF16),
            vmem((8, COLS, 128), BF16),
            vmem((6, COLS, 128), BF16),
            vmem((4, COLS, 128), BF16),
            vmem((COLS, 128), BF16),
            vmem((4, 8, ROWS), F32),
            vmem((10, 8, COLS), F32),
            vmem((BLOCK, COLS), F32),
            pltpu.SemaphoreType.DMA((NSEM,)),
            pltpu.SemaphoreType.DMA((NSEM,)),
            pltpu.SemaphoreType.DMA((16,)),
        ],
        compiler_params=pltpu.CompilerParams(
            collective_id=0, has_side_effects=True, vmem_limit_bytes=62 << 20
        ),
        cost_estimate=pl.CostEstimate(flops=flops, bytes_accessed=16 << 20, transcendentals=0),
        name="kmeans_step",
    )(descriptors, landmarks, whitening, centroids)


def solution(mesh):
    in_specs = (P("blk", None), P("blk", None), P("blk", "cent"), P("cent", None))
    out_specs = (P("blk", "cent"), P("blk", "cent"))
    return jax.shard_map(
        per_device, mesh=mesh, in_specs=in_specs, out_specs=out_specs, check_vma=False
    )
```

```python
import math

import jax
import jax.numpy as jnp
from jax import lax
from jax.experimental import pallas as pl
from jax.experimental.pallas import tpu as pltpu
from jax.sharding import PartitionSpec as P

MESH = pl.DeviceIdType.MESH
F32 = jnp.float32
BF16 = jnp.bfloat16

ROWS = 768
DEPTH = 1024
BLOCK = 128
SUB = 64
HALF_B = 256
GROUP = 4 * BLOCK
LAND = 8 * GROUP
HALF = 512
PIECE = 256
CHUNKS = 4
WCHUNKS = 8
PART = 256
COLS = 1024
NSEM = 224


def dot(a, b, ca, cb):
    return lax.dot_general(a, b, (((ca,), (cb,)), ((), ())), preferred_element_type=F32)


def normalized(values):
    wide = values.astype(F32)
    sum_sq = jnp.sum(wide * wide, axis=1, keepdims=True)
    return (wide * lax.rsqrt(sum_sq + 1e-06)).astype(BF16)


def body(
    desc_hbm, land_hbm, white_hbm, cent_hbm, assign_hbm, out_hbm,
    desc, seed, wseed, land, white, kern, feat, cent, logit, assign_t,
    recv1, part1, recv2, stat, count, out_v,
    send_sem, recv_sem, local_sem, free_sem,
):
    blk, col = lax.axis_index("blk"), lax.axis_index("cent")
    y_lo, x, z = blk // 16, (blk // 4) % 4, blk % 4
    y_hi, core = col // 2, col % 2
    y = y_hi * 2 + y_lo
    away = (y_lo + core) % 2
    is_away, is_home = away == 1, away == 0

    def device(xx, yy, zz, cc):
        xx, yy, zz, cc = xx % 4, yy % 4, zz % 4, cc % 2
        return {"blk": (yy % 2) * 16 + xx * 4 + zz, "cent": (yy // 2) * 2 + cc}

    def on_a(d):
        return device(x + (1 - core) * (d + 4), y, z + core * (d + 4), core)

    def on_b(d):
        return device(x + core * (d + 4), y, z + (1 - core) * (d + 4), core)

    pa = x * (1 - core) + z * core
    pb = z * (1 - core) + x * core
    sibling = device(x, y, z, core + 1)
    swap_y = y + 1 - 2 * y_lo
    swap = device(x, swap_y, z, core + 1)
    other = device(x, 7 - y, z, core + 1)
    y_up, y_down = device(x, y + 1, z, core), device(x, y + 3, z, core)
    y_far, y_far_sib = device(x, y + 2, z, core), device(x, y + 2, z, core + 1)
    y_pair, other_same = device(x, swap_y, z, core), device(x, 7 - y, z, core)

    started = []
    counter = [0]

    def wait_send(c):
        for i, (other_copy, cond) in enumerate(started):
            if other_copy is c:
                del started[i]
                if cond is None:
                    c.wait_send()
                else:
                    pl.when(cond)(c.wait_send)
                return

    def copy(src, dst, target, cond=None):
        k = counter[0]
        counter[0] += 1
        c = pltpu.make_async_remote_copy(
            src_ref=src, dst_ref=dst, send_sem=send_sem.at[k], recv_sem=recv_sem.at[k],
            device_id=target, device_id_type=MESH,
        )
        started.append((c, cond))
        return c

    def when(cond, f):
        pl.when(cond)(f)

    load_seed = pltpu.make_async_copy(land_hbm, seed, local_sem.at[0])
    load_desc = pltpu.make_async_copy(desc_hbm, desc.at[0], local_sem.at[1])
    load_seed.start()
    load_desc.start()
    load_cent = [
        pltpu.make_async_copy(cent_hbm.at[:, pl.ds(p * HALF, HALF)], cent.at[p], local_sem.at[2 + p])
        for p in range(8)
    ]
    load_white = [
        pltpu.make_async_copy(white_hbm.at[:, pl.ds(k * PIECE, PIECE)], wseed.at[k], local_sem.at[10 + k])
        for k in range(CHUNKS)
    ]
    for c in load_white:
        c.start()

    barrier = pltpu.get_barrier_semaphore()
    partners = [
        sibling, on_a(1), on_a(-1), on_a(2), on_b(1), on_b(-1), on_b(2),
        y_up, y_down, y_far, y_far_sib, swap, other,
    ]
    for target in partners:
        pl.semaphore_signal(barrier, inc=1, device_id=target, device_id_type=MESH)

    load_seed.wait()
    seed[...] = normalized(seed[...])
    mine = pl.ds(pl.multiple_of(core * SUB, SUB), SUB)
    theirs = pl.ds(pl.multiple_of((1 - core) * SUB, SUB), SUB)
    land[pl.ds(0, SUB), :] = seed[mine, :]

    pl.semaphore_wait(barrier, len(partners))

    swap_land = copy(seed.at[mine], land.at[pl.ds(HALF_B, SUB)], y_pair)

    def white_seed(quarter, part, rows, target, cond):
        return copy(
            wseed.at[:, rows], white.at[pl.ds(quarter * CHUNKS, CHUNKS), pl.ds(part * HALF_B, SUB)], target, cond
        )

    seed_own = pltpu.make_async_copy(
        wseed.at[:, mine], white.at[pl.ds(0, CHUNKS), pl.ds(0, SUB)], local_sem.at[15]
    )
    seed_sib = white_seed(0, 0, theirs, sibling, is_home)
    seed_pair = white_seed(0, 1, mine, y_pair, is_away)
    seed_swap = white_seed(0, 1, theirs, swap, is_away)
    seed_far = white_seed(1, 0, mine, y_far, is_home)
    seed_far_sib = white_seed(1, 0, theirs, y_far_sib, is_home)
    seed_other = white_seed(1, 1, theirs, other, is_away)
    seed_other_same = white_seed(1, 1, mine, other_same, is_away)
    CUT = 256
    share_cent = [
        copy(cent_hbm.at[:, pl.ds(p * HALF, HALF)], cent.at[p], sibling, is_home) for p in range(8)
    ]
    swap_desc = [
        copy(desc.at[0, pl.ds(0, CUT)], desc.at[1, pl.ds(0, CUT)], swap, is_away),
        copy(desc.at[0, pl.ds(CUT, ROWS - CUT)], desc.at[1, pl.ds(CUT, ROWS - CUT)], other, is_away),
    ]

    class Ring:
        def __init__(self, at, size, to):
            def go(src, dst, rows, half, d):
                lo = half * (rows // 2)
                n = rows if half == 0 and dst != 2 else rows // 2
                return copy(at(src, lo, n), at(dst, lo, n), to(d))

            self.up = go(0, 3, size, 0, 1)
            self.down = go(0, 1, size, 0, -1)
            self.fwd_up = go(3, 2, size, 0, 1)
            self.fwd_down = go(1, 2, size, 1, -1)

        def start(self):
            self.up.start()
            self.down.start()

        def forward(self):
            self.up.wait_recv()
            self.fwd_up.start()
            self.down.wait_recv()
            self.fwd_down.start()

        def finish(self):
            self.fwd_up.wait_recv()
            self.fwd_down.wait_recv()

    def land_a(part):
        return lambda slot, lo, n: land.at[pl.ds(part * HALF_B + slot * SUB + lo, n)]

    def land_b(first):
        return lambda slot, lo, n: land.at[pl.ds(slot * GROUP + first + lo, n)]

    def white_a(quarter, part):
        return lambda slot, lo, n: white.at[
            pl.ds(quarter * CHUNKS, CHUNKS), pl.ds(part * HALF_B + slot * SUB + lo, n)
        ]

    def white_b(k):
        return lambda slot, lo, n: white.at[k, pl.ds(slot * GROUP + lo, n)]

    def to_sibling(at, slot):
        return copy(at(slot, 0, GROUP), at(4 + slot, 0, GROUP), sibling)

    la = [Ring(land_a(part), SUB, on_a) for part in range(2)]
    lb = [Ring(land_b(s * SUB), SUB, on_b) for s in range(4)]
    lb_rest = Ring(land_b(HALF_B), HALF_B, on_b)
    wa = [[Ring(white_a(q, part), SUB, on_a) for part in range(2)] for q in range(2)]
    wb = [Ring(white_b(k), GROUP, on_b) for k in range(WCHUNKS)]
    ls = [to_sibling(land_b(0), s) for s in range(4)]
    ws = [[to_sibling(white_b(k), s) for s in range(4)] for k in range(WCHUNKS)]

    swap_land.start()
    la[0].start()
    lb[0].start()
    for c in load_white:
        c.wait()

    @pl.when(is_home)
    def _():
        seed_own.start()
        seed_sib.start()

    @pl.when(is_away)
    def _():
        seed_pair.start()
        seed_swap.start()

    load_desc.wait()

    @pl.loop(0, 3)
    def _(i):
        s = pl.ds(pl.multiple_of(i * 256, 256), 256)
        desc[0, s, :] = normalized(desc[0, s, :])

    @pl.when(is_away)
    def _():
        swap_desc[0].start()
        swap_desc[1].start()
        seed_other.start()
        seed_other_same.start()

    @pl.when(is_home)
    def _():
        seed_far.start()
        seed_far_sib.start()
        for c in load_cent + share_cent:
            c.start()

    sharpness = math.sqrt(DEPTH)

    def kernel_group(g):
        cols = pl.ds(g * GROUP, GROUP)
        cosine = dot(desc[away], land[cols, :], 1, 1)
        kern[:, cols] = jnp.exp(sharpness * cosine).astype(BF16)

    la[0].up.wait_recv()
    la[0].fwd_up.start()
    lb[3].start()
    la[0].down.wait_recv()
    la[0].fwd_down.start()
    lb[1].start()
    swap_land.wait_recv()
    la[1].start()
    lb[0].forward()
    la[0].finish()
    lb[2].start()
    lb[3].forward()
    lb[1].forward()
    la[1].forward()

    @pl.when(is_home)
    def _():
        seed_own.wait()
        seed_pair.wait_recv()

    @pl.when(is_away)
    def _():
        seed_sib.wait_recv()
        seed_swap.wait_recv()

    for ring in wa[0]:
        ring.start()
    lb[2].forward()
    la[1].finish()
    lb_rest.start()
    ls[0].start()

    @pl.when(is_away)
    def _():
        swap_desc[0].wait_recv()
        swap_desc[1].wait_recv()

    kernel_group(0)
    for ring in wa[0]:
        ring.forward()
    for ring in lb:
        ring.finish()
    lb_rest.forward()
    ls[3].start()
    ls[1].start()
    for ring in wa[0]:
        ring.finish()

    def start_white(k):
        wb[k].start()
        ws[k][0].start()

    def forward_white(k):
        wb[k].forward()
        ws[k][3].start()
        ws[k][1].start()

    def finish_white(k):
        wb[k].finish()
        ws[k][2].start()

    start_white(0)
    start_white(1)
    kernel_group(3)
    kernel_group(1)
    lb_rest.finish()
    ls[2].start()

    @pl.when(is_home)
    def _():
        seed_far.wait_recv()
        seed_other_same.wait_recv()

    @pl.when(is_away)
    def _():
        seed_far_sib.wait_recv()
        seed_other.wait_recv()

    for ring in wa[1]:
        ring.start()
    ls[0].wait_recv()
    kernel_group(4)
    forward_white(0)
    start_white(2)
    ls[3].wait_recv()
    kernel_group(7)
    ls[1].wait_recv()
    kernel_group(5)
    kernel_group(2)
    finish_white(0)
    for ring in wa[1]:
        ring.forward()
    forward_white(1)
    start_white(3)
    ls[2].wait_recv()
    kernel_group(6)

    def slot_of(r, k):
        return ((y + r) % 4) * CHUNKS + k

    def features(k):
        for s in range(4):
            ws[k][s].wait_recv()
        slot = slot_of(0, k) if k < CHUNKS else slot_of(2, k - CHUNKS)

        @pl.loop(0, 3)
        def _(i):
            s = pl.ds(pl.multiple_of(i * 256, 256), 256)
            feat[slot, s, :] = dot(kern[s, :], white[k], 1, 0).astype(BF16)

    own = [feat.at[slot_of(0, k)] for k in range(CHUNKS)]
    f_up = [copy(own[k], own[k], y_up) for k in range(CHUNKS)]
    f_down = [copy(own[k], own[k], y_down) for k in range(CHUNKS)]

    def logits(r, k):
        if r == 1:
            f_down[k].wait_recv()
        if r == 3:
            f_up[k].wait_recv()
        lanes = pl.ds((k % 2) * PIECE, PIECE)
        slot, piece = ((y + r) % 4) * 2 + k // 2, slot_of(r, k)

        @pl.loop(0, 2)
        def _(i):
            s = pl.ds(pl.multiple_of(i * 512, 512), 512)
            update = dot(cent[slot, s, lanes], feat[piece], 1, 1)
            if k == 0 and r == 0:
                logit[s, :] = update
            else:
                logit[s, :] += update

    features(0)
    f_up[0].start()
    f_down[0].start()
    for k in range(1, CHUNKS):
        finish_white(k)
        if k == 1:
            for ring in wa[1]:
                ring.finish()
        forward_white(k + 1)
        start_white(k + 3)
        features(k)
        f_up[k].start()
        f_down[k].start()

    @pl.when(is_home)
    def _():
        for c in load_cent:
            c.wait()

    @pl.when(is_away)
    def _():
        for c in share_cent:
            c.wait_recv()

    todo = [
        [(0, 0), (0, 1)],
        [(0, 2), (0, 3), (2, 0)],
        [(1, 0), (3, 0), (2, 1)],
        [(1, 1), (3, 1), (2, 2), (1, 2), (3, 2), (2, 3), (1, 3), (3, 3)],
    ]
    for k in range(CHUNKS, WCHUNKS):
        finish_white(k)
        if k + 1 < WCHUNKS:
            forward_white(k + 1)
        if k + 3 < WCHUNKS:
            start_white(k + 3)
        features(k)
        for r, piece in todo[k - CHUNKS]:
            logits(r, piece)

    for ring in la + lb + [lb_rest]:
        for c in (ring.up, ring.down, ring.fwd_up, ring.fwd_down):
            wait_send(c)
    for c in ls:
        wait_send(c)
    pl.semaphore_signal(free_sem, inc=1, device_id=sibling, device_id_type=MESH)

    def quarter(i):
        return pl.ds(pl.multiple_of(i * 256, 256), 256)

    def highest(i, top):
        return jnp.maximum(top, jnp.max(logit[quarter(i), :], axis=0, keepdims=True))

    top = lax.fori_loop(0, 4, highest, jnp.full((1, ROWS), -jnp.inf, F32))

    def exponentials(i, total):
        weights = jnp.exp(logit[quarter(i), :] - top)
        logit[quarter(i), :] = weights
        return total + jnp.sum(weights, axis=0, keepdims=True)

    total = lax.fori_loop(0, 4, exponentials, jnp.zeros((1, ROWS), F32))
    stat[0, 0:1, :] = top
    stat[0, 1:2, :] = total
    stat_copies = [
        copy(stat.at[0], stat.at[i + 1], target)
        for i, target in enumerate((y_up, y_down, y_far))
    ]
    for c in stat_copies:
        c.start()
    for c in stat_copies:
        c.wait_recv()
    tops = [stat[i, 0:1, :] for i in range(4)]
    all_top = jnp.maximum(jnp.maximum(tops[0], tops[1]), jnp.maximum(tops[2], tops[3]))
    all_total = sum(stat[i, 1:2, :] * jnp.exp(tops[i] - all_top) for i in range(4))
    factor = jnp.exp(tops[0] - all_top) / all_total

    @pl.loop(0, 4)
    def _(i):
        assign_t[quarter(i), :] = (logit[quarter(i), :] * factor).astype(BF16)

    def partial_sum(slot, ta, owner, i):
        ta = ta % 4
        parts = []
        for b in range(4):
            xb = (1 - owner) * ta + owner * b
            zb = (1 - owner) * b + owner * ta
            lanes = pl.ds(pl.multiple_of((zb % 2) * 128, 128), 128)
            parts.append(feat[(owner * 4 + xb) * 2 + zb // 2, :, lanes])
        s = pl.ds(i * 512, 512)
        cent[slot, s, :] = dot(assign_t[s, :], jnp.concatenate(parts, axis=1), 1, 0).astype(BF16)

    def add(*values):
        total = values[0].astype(F32)
        for v in values[1:]:
            total = total + v.astype(F32)
        return total

    FAR, UP, DOWN, OWN = range(4)
    offsets = (2, 1, 3, 0)
    landing = [land.at[pl.ds(t * COLS, COLS), pl.ds(0, HALF)] for t in range(4)]
    halves = [
        [copy(cent.at[4 + t, rows], landing[t].at[rows], sibling) for rows in (pl.ds(0, 512), pl.ds(512, 512))]
        for t in range(4)
    ]

    def chunk(half, i):
        return pl.ds(half * 512 + i * PART, PART)

    class RingSum:
        def __init__(self, at, landing, to, i):
            self.rows = [chunk(half, i) for half in range(2)]
            self.x, self.y, self.z = [], [], []
            for half in range(2):
                r = self.rows[half]
                ahead, back = (UP, DOWN) if half == 0 else (DOWN, UP)
                d = 1 - 2 * half
                self.x.append(copy(at(FAR, r), landing.at[0, r], to(d)))
                self.z.append(copy(at(ahead, r), landing.at[1, r], to(d)))
                self.y.append(copy(at(back, r), landing.at[2, r], to(-d)))

    PAIRS = 2
    places = [(pb + d) % 4 for d in offsets]
    rs1 = [RingSum(lambda t, r: cent.at[t, r], recv1, on_a, i) for i in range(PAIRS)]
    direct = [
        [
            copy(part1.at[places[t], chunk(half, i)], recv2.at[t, chunk(half, i)], on_b(offsets[t]))
            for t in (FAR, UP, DOWN)
            for half in range(2)
        ]
        for i in range(PAIRS)
    ]

    def start_both(copies):
        for c in copies:
            c.start()

    def make_half(t):
        for i in range(2):
            partial_sum(4 + t, pb + offsets[t], 1 - core, i)
            halves[t][i].start()
        for i in range(2):
            partial_sum(t, pa + offsets[t], core, i)

    def merge(t, half):
        halves[t][half].wait_recv()

        @pl.loop(2 * half, 2 * half + 2)
        def _(i):
            came = land[pl.ds(pl.multiple_of(t * COLS + i * 256, 256), 256), pl.ds(0, HALF)]
            cent[t, quarter(i), :] = add(cent[t, quarter(i), :], came).astype(BF16)

    ones = jnp.ones((8, ROWS), BF16)
    count[0] = dot(ones, assign_t[...], 1, 1)
    count_s = copy(count.at[0], count.at[1], sibling)
    count_a = [copy(count.at[2], count.at[3 + i], on_a(d)) for i, d in enumerate((1, -1, 2))]
    count_b = [copy(count.at[6], count.at[7 + i], on_b(d)) for i, d in enumerate((1, -1, 2))]

    pl.semaphore_wait(free_sem, 1)
    make_half(FAR)
    for half in range(2):
        merge(FAR, half)
        rs1[0].x[half].start()
        rs1[1].x[half].start()
    count_s.start()
    make_half(UP)
    make_half(DOWN)
    for t in (UP, DOWN):
        for half in range(2):
            merge(t, half)
    start_both(rs1[0].y)

    def turn1(i):
        for half, t in ((0, UP), (1, DOWN)):
            r = rs1[i].rows[half]
            rs1[i].x[half].wait_recv()
            cent[t, r, :] = add(cent[t, r, :], recv1[0, r, :]).astype(BF16)
            rs1[i].z[half].start()

    def end1(i):
        for half in range(2):
            r = rs1[i].rows[half]
            rs1[i].y[half].wait_recv()
            rs1[i].z[half].wait_recv()
            total = add(cent[OWN, r, :], recv1[1, r, :], recv1[2, r, :]).astype(BF16)
            for b in range(4):
                part1[b, r, :] = total[:, b * 128 : (b + 1) * 128]
        start_both(direct[i])

    send_out = [
        [copy(out_v.at[:, chunk(half, i)], out_hbm.at[:, chunk(half, i)], swap, is_away) for half in range(2)]
        for i in range(PAIRS)
    ]
    store_out = [
        [pltpu.make_async_copy(out_v.at[:, chunk(half, i)], out_hbm.at[:, chunk(half, i)], local_sem.at[16 + 2 * i + half])
         for half in range(2)]
        for i in range(PAIRS)
    ]

    def end2(i):
        for c in direct[i]:
            c.wait_recv()
        for half in range(2):
            r = chunk(half, i)
            sums = add(part1[pb, r, :], recv2[0, r, :], recv2[1, r, :], recv2[2, r, :])
            counts = count[6, 0:1, r] + count[7, 0:1, r] + count[8, 0:1, r] + count[9, 0:1, r]
            out_v[:, r] = sums.T / jnp.maximum(counts, 1.0)
            when(is_home, store_out[i][half].start)
            when(is_away, send_out[i][half].start)

    turn1(0)
    start_both(rs1[1].y)
    count_s.wait_recv()
    count[2] = count[0] + count[1]
    start_both(count_a)
    make_half(OWN)
    turn1(1)

    @pl.when(is_away)
    def _():
        swap_desc[0].wait_send()
        swap_desc[1].wait_send()

    @pl.loop(0, 6)
    def _(i):
        s = pl.ds(pl.multiple_of(i * 128, 128), 128)
        desc[0, s, :] = assign_t[:, s].T

    store_assign = pltpu.make_async_copy(desc.at[0], assign_hbm, local_sem.at[14])
    send_assign = copy(desc.at[0], assign_hbm, swap, is_away)
    when(is_home, store_assign.start)
    when(is_away, send_assign.start)
    for c in count_a:
        c.wait_recv()
    count[6] = count[2] + count[3] + count[4] + count[5]
    start_both(count_b)
    merge(OWN, 0)
    merge(OWN, 1)
    end1(0)
    for c in count_b:
        c.wait_recv()
    end1(1)
    end2(0)
    end2(1)

    for c, cond in started:
        if any(c is d for d in swap_desc):
            continue
        if cond is None:
            c.wait_send()
        else:
            when(cond, lambda c=c: c.wait_send())

    @pl.when(is_home)
    def _():
        store_assign.wait()
        for pair in store_out:
            for c in pair:
                c.wait()

    @pl.when(is_away)
    def _():
        send_assign.wait_recv()
        for pair in send_out:
            for c in pair:
                c.wait_recv()


def per_device(descriptors, landmarks, whitening, centroids):
    vmem = pltpu.VMEM
    hbm = pl.BlockSpec(memory_space=pl.ANY)
    flops = 2 * ROWS * LAND * DEPTH * 4
    return pl.pallas_call(
        body,
        out_shape=(
            jax.ShapeDtypeStruct((ROWS, COLS), BF16),
            jax.ShapeDtypeStruct((BLOCK, COLS), F32),
        ),
        in_specs=[hbm] * 4,
        out_specs=(hbm, hbm),
        scratch_shapes=[
            vmem((2, ROWS, DEPTH), BF16),
            vmem((BLOCK, DEPTH), BF16),
            vmem((CHUNKS, BLOCK, PIECE), BF16),
            vmem((LAND, DEPTH), BF16),
            vmem((WCHUNKS, LAND, PIECE), BF16),
            vmem((ROWS, LAND), BF16),
            vmem((16, ROWS, PIECE), BF16),
            vmem((8, COLS, HALF), BF16),
            vmem((COLS, ROWS), F32),
            vmem((COLS, ROWS), BF16),
            vmem((3, COLS, HALF), BF16),
            vmem((4, COLS, 128), BF16),
            vmem((3, COLS, 128), BF16),
            vmem((4, 8, ROWS), F32),
            vmem((10, 8, COLS), F32),
            vmem((BLOCK, COLS), F32),
            pltpu.SemaphoreType.DMA((NSEM,)),
            pltpu.SemaphoreType.DMA((NSEM,)),
            pltpu.SemaphoreType.DMA((20,)),
            pltpu.SemaphoreType.REGULAR,
        ],
        compiler_params=pltpu.CompilerParams(
            collective_id=0, has_side_effects=True, vmem_limit_bytes=62 << 20
        ),
        cost_estimate=pl.CostEstimate(flops=flops, bytes_accessed=16 << 20, transcendentals=0),
        name="kmeans_step",
    )(descriptors, landmarks, whitening, centroids)


def solution(mesh):
    in_specs = (P("blk", None), P("blk", None), P("blk", "cent"), P("cent", None))
    out_specs = (P("blk", "cent"), P("blk", "cent"))
    return jax.shard_map(
        per_device, mesh=mesh, in_specs=in_specs, out_specs=out_specs, check_vma=False
    )
```

```python
import math

import jax
import jax.numpy as jnp
from jax import lax
from jax.experimental import pallas as pl
from jax.experimental.pallas import tpu as pltpu
from jax.sharding import PartitionSpec as P

MESH = pl.DeviceIdType.MESH
F32 = jnp.float32
BF16 = jnp.bfloat16

ROWS = 768
DEPTH = 1024
BLOCK = 128
SUB = 64
HALF_B = 256
GROUP = 4 * BLOCK
LAND = 8 * GROUP
HALF = 512
PIECE = 256
CHUNKS = 4
WCHUNKS = 8
PART = 256
COLS = 1024
NSEND = 64
NRECV = 116


def dot(a, b, ca, cb):
    return lax.dot_general(a, b, (((ca,), (cb,)), ((), ())), preferred_element_type=F32)


def normalized(values):
    wide = values.astype(F32)
    sum_sq = jnp.sum(wide * wide, axis=1, keepdims=True)
    return (wide * lax.rsqrt(sum_sq + 1e-06)).astype(BF16)


def body(
    desc_hbm, land_hbm, white_hbm, cent_hbm, assign_hbm, out_hbm,
    desc, seed, wseed, land, white, kern, feat, cent, logit, assign_t,
    recv1, part1, recv2, stat, count, out_v,
    send_sem, recv_sem, local_sem, free_sem,
):
    blk, col = lax.axis_index("blk"), lax.axis_index("cent")
    y_lo, x, z = blk // 16, (blk // 4) % 4, blk % 4
    y_hi, core = col // 2, col % 2
    y = y_hi * 2 + y_lo
    away = (y_lo + core) % 2
    is_away, is_home = away == 1, away == 0

    def device(xx, yy, zz, cc):
        xx, yy, zz, cc = xx % 4, yy % 4, zz % 4, cc % 2
        return {"blk": (yy % 2) * 16 + xx * 4 + zz, "cent": (yy // 2) * 2 + cc}

    def on_a(d):
        return device(x + (1 - core) * (d + 4), y, z + core * (d + 4), core)

    def on_b(d):
        return device(x + core * (d + 4), y, z + (1 - core) * (d + 4), core)

    pa = x * (1 - core) + z * core
    pb = z * (1 - core) + x * core
    sibling = device(x, y, z, core + 1)
    swap_y = y + 1 - 2 * y_lo
    swap = device(x, swap_y, z, core + 1)
    other = device(x, 7 - y, z, core + 1)
    y_up, y_down = device(x, y + 1, z, core), device(x, y + 3, z, core)
    y_far, y_far_sib = device(x, y + 2, z, core), device(x, y + 2, z, core + 1)
    y_pair, other_same = device(x, swap_y, z, core), device(x, 7 - y, z, core)

    free_sends = list(range(NSEND))[::-1]
    counter = [0]
    live = []

    def new_recv():
        counter[0] += 1
        return counter[0] - 1

    def describe(src, dst, send, recv, target):
        return pltpu.make_async_remote_copy(
            src_ref=src, dst_ref=dst, send_sem=send_sem.at[send], recv_sem=recv_sem.at[recv],
            device_id=target, device_id_type=MESH,
        )

    class Copy:
        def __init__(self, src, dst, target, cond=None, recv=None):
            self.parts = src, dst
            self.target, self.cond = target, cond
            self.recv = new_recv() if recv is None else recv

        def start(self):
            self.send = free_sends.pop()
            live.append(self)
            describe(*self.parts, self.send, self.recv, self.target).start()

        def wait_recv(self):
            describe(*self.parts, 0, self.recv, self.target).wait_recv()

        def wait_send(self):
            wait = describe(*self.parts, self.send, self.recv, self.target).wait_send
            if self.cond is None:
                wait()
            else:
                pl.when(self.cond)(wait)
            live.remove(self)
            free_sends.append(self.send)

    class Group(Copy):
        def __init__(self, members, whole, target, cond=None):
            super().__init__(*whole, target, cond)
            self.members = members
            self.left = len(members)

        def start(self, i=None):
            if self.left == len(self.members):
                self.send = free_sends.pop()
                live.append(self)
            for src, dst, target in self.members if i is None else [self.members[i]]:
                self.left -= 1
                describe(src, dst, self.send, self.recv, target).start()

    copy = Copy

    def retire(copies):
        for c in copies:
            c.wait_send()

    def when(cond, f):
        pl.when(cond)(f)

    load_seed = pltpu.make_async_copy(land_hbm, seed, local_sem.at[0])
    load_desc = pltpu.make_async_copy(desc_hbm, desc.at[0], local_sem.at[1])
    load_seed.start()
    load_desc.start()
    load_cent = [
        pltpu.make_async_copy(cent_hbm.at[:, pl.ds(p * HALF, HALF)], cent.at[p], local_sem.at[2 + p])
        for p in range(8)
    ]
    load_white = [
        pltpu.make_async_copy(white_hbm.at[:, pl.ds(k * PIECE, PIECE)], wseed.at[k], local_sem.at[10 + k])
        for k in range(CHUNKS)
    ]
    for c in load_white:
        c.start()

    barrier = pltpu.get_barrier_semaphore()
    partners = [
        sibling, on_a(1), on_a(-1), on_a(2), on_b(1), on_b(-1), on_b(2),
        y_up, y_down, y_far, y_far_sib, swap, other,
    ]
    for target in partners:
        pl.semaphore_signal(barrier, inc=1, device_id=target, device_id_type=MESH)

    load_seed.wait()
    seed[...] = normalized(seed[...])
    mine = pl.ds(pl.multiple_of(core * SUB, SUB), SUB)
    theirs = pl.ds(pl.multiple_of((1 - core) * SUB, SUB), SUB)
    land[pl.ds(0, SUB), :] = seed[mine, :]

    pl.semaphore_wait(barrier, len(partners))

    swap_land = copy(seed.at[mine], land.at[pl.ds(HALF_B, SUB)], y_pair)

    widths = (CHUNKS, WCHUNKS - CHUNKS)

    def white_seed(quarter, part, rows, target, cond):
        return copy(
            wseed.at[pl.ds(0, widths[quarter]), rows],
            white.at[pl.ds(quarter * CHUNKS, widths[quarter]), pl.ds(part * HALF_B, SUB)], target, cond,
        )

    seed_own = pltpu.make_async_copy(
        wseed.at[:, mine], white.at[pl.ds(0, CHUNKS), pl.ds(0, SUB)], local_sem.at[15]
    )
    seed_sib = white_seed(0, 0, theirs, sibling, is_home)
    seed_pair = white_seed(0, 1, mine, y_pair, is_away)
    seed_swap = white_seed(0, 1, theirs, swap, is_away)
    seed_far = white_seed(1, 0, mine, y_far, is_home)
    seed_far_sib = white_seed(1, 0, theirs, y_far_sib, is_home)
    seed_other = white_seed(1, 1, theirs, other, is_away)
    seed_other_same = white_seed(1, 1, mine, other_same, is_away)
    CUT = 256
    share_cent = Group(
        [(cent_hbm.at[:, pl.ds(p * HALF, HALF)], cent.at[p], sibling) for p in range(8)],
        (cent, cent), sibling, is_home,
    )
    swap_desc = [
        copy(desc.at[0, pl.ds(0, CUT)], desc.at[1, pl.ds(0, CUT)], swap, is_away),
        copy(desc.at[0, pl.ds(CUT, ROWS - CUT)], desc.at[1, pl.ds(CUT, ROWS - CUT)], other, is_away),
    ]

    class Ring:
        def __init__(self, at, size, to, direct=False):
            half = size // 2
            self.up = copy(at(0, 0, size), at(3, 0, size), to(1))
            self.down = copy(at(0, 0, size), at(1, 0, size), to(-1))
            if direct:
                self.far = copy(at(0, 0, size), at(2, 0, size), to(2))
                self.copies = [self.up, self.down, self.far]
                return
            self.fwd_up = copy(at(3, 0, half), at(2, 0, half), to(1))
            self.fwd_down = copy(at(1, half, half), at(2, half, half), to(-1), recv=self.fwd_up.recv)
            self.both = copy(at(0, 0, size), at(2, 0, size), to(1), recv=self.fwd_up.recv)
            self.copies = [self.up, self.down, self.fwd_up, self.fwd_down]

        def start(self):
            self.up.start()
            self.down.start()

        def forward(self):
            self.up.wait_recv()
            self.fwd_up.start()
            self.down.wait_recv()
            self.fwd_down.start()

        def finish(self):
            self.both.wait_recv()

    def land_a(part):
        return lambda slot, lo, n: land.at[pl.ds(part * HALF_B + slot * SUB + lo, n)]

    def land_b(first):
        return lambda slot, lo, n: land.at[pl.ds(slot * GROUP + first + lo, n)]

    def white_a(quarter, part):
        return lambda slot, lo, n: white.at[
            pl.ds(quarter * CHUNKS, widths[quarter]), pl.ds(part * HALF_B + slot * SUB + lo, n)
        ]

    def white_b(k):
        return lambda slot, lo, n: white.at[k, pl.ds(slot * GROUP + lo, n)]

    la = [Ring(land_a(part), SUB, on_a, True) for part in range(2)]
    lb = [Ring(land_b(s * SUB), SUB, on_b) for s in range(4)]
    lb_rest = Ring(land_b(HALF_B), HALF_B, on_b)
    wa = [[Ring(white_a(q, part), SUB, on_a) for part in range(2)] for q in range(2)]
    wb = [Ring(white_b(k), GROUP, on_b) for k in range(WCHUNKS)]
    ls = [copy(land_b(0)(s, 0, GROUP), land_b(0)(4 + s, 0, GROUP), sibling) for s in range(4)]
    ws = [
        Group(
            [(white_b(k)(s, 0, GROUP), white_b(k)(4 + s, 0, GROUP), sibling) for s in range(4)],
            (white_b(k)(0, 0, 4 * GROUP), white_b(k)(4, 0, 4 * GROUP)), sibling,
        )
        for k in range(WCHUNKS)
    ]

    swap_land.start()
    la[0].start()
    la[0].far.start()
    lb[0].start()
    for c in load_white:
        c.wait()

    @pl.when(is_home)
    def _():
        seed_own.start()
        seed_sib.start()

    @pl.when(is_away)
    def _():
        seed_pair.start()
        seed_swap.start()

    load_desc.wait()

    @pl.loop(0, 3)
    def _(i):
        s = pl.ds(pl.multiple_of(i * 256, 256), 256)
        desc[0, s, :] = normalized(desc[0, s, :])

    @pl.when(is_away)
    def _():
        swap_desc[0].start()
        swap_desc[1].start()
        seed_other.start()
        seed_other_same.start()

    @pl.when(is_home)
    def _():
        seed_far.start()
        seed_far_sib.start()
        for c in load_cent:
            c.start()
        share_cent.start()

    sharpness = math.sqrt(DEPTH)

    def kernel_group(g):
        cols = pl.ds(g * GROUP, GROUP)
        cosine = dot(desc[away], land[cols, :], 1, 1)
        kern[:, cols] = jnp.exp(sharpness * cosine).astype(BF16)

    la[0].up.wait_recv()
    lb[3].start()
    la[0].down.wait_recv()
    lb[1].start()
    la[0].far.wait_recv()
    lb[2].start()
    swap_land.wait_recv()
    la[1].start()
    la[1].far.start()
    lb[0].forward()

    @pl.when(is_home)
    def _():
        seed_own.wait()
        seed_pair.wait_recv()

    @pl.when(is_away)
    def _():
        seed_sib.wait_recv()
        seed_swap.wait_recv()

    for ring in wa[0]:
        ring.start()
    for c in la[1].copies:
        c.wait_recv()
    lb_rest.start()
    ls[0].start()
    lb[3].forward()
    lb[1].forward()
    lb[2].forward()
    for ring in wa[0]:
        ring.forward()

    @pl.when(is_away)
    def _():
        swap_desc[0].wait_recv()
        swap_desc[1].wait_recv()

    kernel_group(0)
    for ring in lb:
        ring.finish()
    lb_rest.forward()
    ls[3].start()
    ls[1].start()
    for ring in wa[0]:
        ring.finish()

    def start_white(k):
        wb[k].start()
        ws[k].start(0)

    def forward_white(k):
        wb[k].forward()
        ws[k].start(3)
        ws[k].start(1)

    def finish_white(k):
        wb[k].finish()
        ws[k].start(2)

    start_white(0)
    kernel_group(3)
    start_white(1)
    kernel_group(1)
    lb_rest.finish()
    ls[2].start()

    @pl.when(is_home)
    def _():
        seed_far.wait_recv()
        seed_other_same.wait_recv()

    @pl.when(is_away)
    def _():
        seed_far_sib.wait_recv()
        seed_other.wait_recv()

    for ring in wa[1]:
        ring.start()
    ls[0].wait_recv()
    kernel_group(4)
    forward_white(0)
    start_white(2)
    ls[3].wait_recv()
    kernel_group(7)
    ls[1].wait_recv()
    kernel_group(5)
    kernel_group(2)
    finish_white(0)
    retire([swap_land, seed_sib, seed_pair, seed_swap, seed_far, seed_far_sib, seed_other, seed_other_same])
    retire([c for ring in la + lb + [lb_rest] + wa[0] for c in ring.copies])
    for ring in wa[1]:
        ring.forward()
    forward_white(1)
    start_white(3)
    ls[2].wait_recv()
    kernel_group(6)

    def slot_of(r, k):
        return ((y + r) % 4) * CHUNKS + k

    def features(k):
        ws[k].wait_recv()
        slot = slot_of(0, k) if k < CHUNKS else slot_of(2, k - CHUNKS)

        @pl.loop(0, 3)
        def _(i):
            s = pl.ds(pl.multiple_of(i * 256, 256), 256)
            feat[slot, s, :] = dot(kern[s, :], white[k], 1, 0).astype(BF16)

        if k > 0:
            retire(wb[k - 1].copies + [ws[k - 1]])

    own = [feat.at[slot_of(0, k)] for k in range(CHUNKS)]
    f_up = [copy(own[k], own[k], y_up) for k in range(CHUNKS)]
    f_down = [copy(own[k], own[k], y_down) for k in range(CHUNKS)]

    begun = []

    def logits(pieces):
        terms = []
        for r, k in pieces:
            if r == 1:
                f_down[k].wait_recv()
            if r == 3:
                f_up[k].wait_recv()
            lanes = pl.ds((k % 2) * PIECE, PIECE)
            terms.append((((y + r) % 4) * 2 + k // 2, lanes, slot_of(r, k)))
        fresh = not begun
        begun.append(True)

        @pl.loop(0, 2)
        def _(i):
            s = pl.ds(pl.multiple_of(i * 512, 512), 512)
            update = sum(dot(cent[slot, s, lanes], feat[piece], 1, 1) for slot, lanes, piece in terms)
            if fresh:
                logit[s, :] = update
            else:
                logit[s, :] += update

    features(0)
    f_up[0].start()
    f_down[0].start()
    for k in range(1, CHUNKS):
        finish_white(k)
        if k == 1:
            for ring in wa[1]:
                ring.finish()
        forward_white(k + 1)
        if k + 3 < WCHUNKS:
            start_white(k + 3)
        features(k)
        f_up[k].start()
        f_down[k].start()

    @pl.when(is_home)
    def _():
        for c in load_cent:
            c.wait()

    @pl.when(is_away)
    def _():
        share_cent.wait_recv()

    early = {7: [[(2, 1), (2, 2)]]}
    late = {
        4: [[(0, 0), (0, 1)], [(0, 2), (0, 3)]],
        5: [[(1, 0), (3, 0), (2, 0)]],
        6: [[(1, 1), (3, 1)]],
        7: [[(1, 2), (3, 2)], [(1, 3), (3, 3), (2, 3)]],
    }
    for k in range(CHUNKS, WCHUNKS):
        finish_white(k)
        if k + 1 < WCHUNKS:
            forward_white(k + 1)
        if k + 3 < WCHUNKS:
            start_white(k + 3)
        for pieces in early.get(k, ()):
            logits(pieces)
        features(k)
        for pieces in late.get(k, ()):
            logits(pieces)

    retire(ls)
    pl.semaphore_signal(free_sem, inc=1, device_id=sibling, device_id_type=MESH)

    def quarter(i):
        return pl.ds(pl.multiple_of(i * 256, 256), 256)

    def highest(i, top):
        return jnp.maximum(top, jnp.max(logit[quarter(i), :], axis=0, keepdims=True))

    top = lax.fori_loop(0, 4, highest, jnp.full((1, ROWS), -jnp.inf, F32))

    def exponentials(i, total):
        weights = jnp.exp(logit[quarter(i), :] - top)
        logit[quarter(i), :] = weights
        return total + jnp.sum(weights, axis=0, keepdims=True)

    total = lax.fori_loop(0, 4, exponentials, jnp.zeros((1, ROWS), F32))
    stat[0, 0:1, :] = top
    stat[0, 1:2, :] = total
    share_stat = Group(
        [(stat.at[0], stat.at[i + 1], target) for i, target in enumerate((y_up, y_down, y_far))],
        (stat.at[pl.ds(1, 3)], stat.at[pl.ds(1, 3)]), y_up,
    )
    share_stat.start()
    share_stat.wait_recv()
    tops = [stat[i, 0:1, :] for i in range(4)]
    all_top = jnp.maximum(jnp.maximum(tops[0], tops[1]), jnp.maximum(tops[2], tops[3]))
    all_total = sum(stat[i, 1:2, :] * jnp.exp(tops[i] - all_top) for i in range(4))
    factor = jnp.exp(tops[0] - all_top) / all_total

    @pl.loop(0, 4)
    def _(i):
        assign_t[quarter(i), :] = (logit[quarter(i), :] * factor).astype(BF16)

    def partial_sum(slot, ta, owner, i):
        ta = ta % 4
        parts = []
        for b in range(4):
            xb = (1 - owner) * ta + owner * b
            zb = (1 - owner) * b + owner * ta
            lanes = pl.ds(pl.multiple_of((zb % 2) * 128, 128), 128)
            parts.append(feat[(owner * 4 + xb) * 2 + zb // 2, :, lanes])
        s = pl.ds(i * 512, 512)
        cent[slot, s, :] = dot(assign_t[s, :], jnp.concatenate(parts, axis=1), 1, 0).astype(BF16)

    def add(*values):
        total = values[0].astype(F32)
        for v in values[1:]:
            total = total + v.astype(F32)
        return total

    FAR, UP, DOWN, OWN = range(4)
    offsets = (2, 1, 3, 0)
    landing = [land.at[pl.ds(t * COLS, COLS), pl.ds(0, HALF)] for t in range(4)]
    halves = [
        [copy(cent.at[4 + t, rows], landing[t].at[rows], sibling) for rows in (pl.ds(0, 512), pl.ds(512, 512))]
        for t in range(4)
    ]

    def chunk(half, i):
        return pl.ds(half * 512 + i * PART, PART)

    class RingSum:
        def __init__(self, at, landing, to, i):
            self.rows = [chunk(half, i) for half in range(2)]
            self.x, self.y, self.z = [], [], []
            for half in range(2):
                r = self.rows[half]
                ahead, back = (UP, DOWN) if half == 0 else (DOWN, UP)
                d = 1 - 2 * half
                self.x.append(copy(at(FAR, r), landing.at[0, r], to(d)))
                self.z.append(copy(at(ahead, r), landing.at[1, r], to(d)))
                self.y.append(copy(at(back, r), landing.at[2, r], to(-d)))

    PAIRS = 2
    places = [(pb + d) % 4 for d in offsets]
    rs1 = [RingSum(lambda t, r: cent.at[t, r], recv1, on_a, i) for i in range(PAIRS)]
    same_size = recv2.at[:, pl.ds(0, 2 * PART)]
    direct = [
        Group(
            [
                (part1.at[places[t], chunk(half, i)], recv2.at[t, chunk(half, i)], on_b(offsets[t]))
                for t in (FAR, UP, DOWN)
                for half in range(2)
            ],
            (same_size, same_size), on_b(1),
        )
        for i in range(PAIRS)
    ]

    def start_both(copies):
        for c in copies:
            c.start()

    def make_half(t):
        for i in range(2):
            partial_sum(4 + t, pb + offsets[t], 1 - core, i)
            halves[t][i].start()
        for i in range(2):
            partial_sum(t, pa + offsets[t], core, i)

    def merge(t, half):
        halves[t][half].wait_recv()

        @pl.loop(2 * half, 2 * half + 2)
        def _(i):
            came = land[pl.ds(pl.multiple_of(t * COLS + i * 256, 256), 256), pl.ds(0, HALF)]
            cent[t, quarter(i), :] = add(cent[t, quarter(i), :], came).astype(BF16)

    ones = jnp.ones((8, ROWS), BF16)
    count[0] = dot(ones, assign_t[...], 1, 1)
    count_s = copy(count.at[0], count.at[1], sibling)
    three = count.at[pl.ds(3, 3)], count.at[pl.ds(3, 3)]
    count_a = Group([(count.at[2], count.at[3 + i], on_a(d)) for i, d in enumerate((1, -1, 2))], three, on_a(1))
    count_b = Group([(count.at[6], count.at[7 + i], on_b(d)) for i, d in enumerate((1, -1, 2))], three, on_b(1))

    pl.semaphore_wait(free_sem, 1)
    make_half(FAR)
    for half in range(2):
        merge(FAR, half)
        rs1[0].x[half].start()
        rs1[1].x[half].start()
    count_s.start()
    make_half(UP)
    make_half(DOWN)
    for t in (UP, DOWN):
        for half in range(2):
            merge(t, half)
    start_both(rs1[0].y)

    def turn1(i):
        for half, t in ((0, UP), (1, DOWN)):
            r = rs1[i].rows[half]
            rs1[i].x[half].wait_recv()
            cent[t, r, :] = add(cent[t, r, :], recv1[0, r, :]).astype(BF16)
            rs1[i].z[half].start()

    def end1(i):
        for half in range(2):
            r = rs1[i].rows[half]
            rs1[i].y[half].wait_recv()
            rs1[i].z[half].wait_recv()
            total = add(cent[OWN, r, :], recv1[1, r, :], recv1[2, r, :]).astype(BF16)
            for b in range(4):
                part1[b, r, :] = total[:, b * 128 : (b + 1) * 128]
        direct[i].start()

    send_out = Group(
        [
            (out_v.at[:, chunk(half, i)], out_hbm.at[:, chunk(half, i)], swap)
            for i in range(PAIRS)
            for half in range(2)
        ],
        (out_v, out_hbm), swap, is_away,
    )
    store_out = [
        [pltpu.make_async_copy(out_v.at[:, chunk(half, i)], out_hbm.at[:, chunk(half, i)], local_sem.at[16 + 2 * i + half])
         for half in range(2)]
        for i in range(PAIRS)
    ]

    def end2(i):
        direct[i].wait_recv()
        for half in range(2):
            r = chunk(half, i)
            sums = add(part1[pb, r, :], recv2[0, r, :], recv2[1, r, :], recv2[2, r, :])
            counts = count[6, 0:1, r] + count[7, 0:1, r] + count[8, 0:1, r] + count[9, 0:1, r]
            out_v[:, r] = sums.T / jnp.maximum(counts, 1.0)
            when(is_home, store_out[i][half].start)
            when(is_away, lambda: send_out.start(2 * i + half))

    turn1(0)
    start_both(rs1[1].y)
    count_s.wait_recv()
    count[2] = count[0] + count[1]
    count_a.start()
    make_half(OWN)
    turn1(1)

    retire(swap_desc)

    @pl.loop(0, 6)
    def _(i):
        s = pl.ds(pl.multiple_of(i * 128, 128), 128)
        desc[0, s, :] = assign_t[:, s].T

    store_assign = pltpu.make_async_copy(desc.at[0], assign_hbm, local_sem.at[14])
    send_assign = copy(desc.at[0], assign_hbm, swap, is_away)
    when(is_home, store_assign.start)
    when(is_away, send_assign.start)
    count_a.wait_recv()
    count[6] = count[2] + count[3] + count[4] + count[5]
    count_b.start()
    merge(OWN, 0)
    merge(OWN, 1)
    end1(0)
    count_b.wait_recv()
    end1(1)
    end2(0)
    end2(1)

    retire(list(live))

    @pl.when(is_home)
    def _():
        store_assign.wait()
        for pair in store_out:
            for c in pair:
                c.wait()

    @pl.when(is_away)
    def _():
        send_assign.wait_recv()
        send_out.wait_recv()


def per_device(descriptors, landmarks, whitening, centroids):
    vmem = pltpu.VMEM
    hbm = pl.BlockSpec(memory_space=pl.ANY)
    flops = 2 * ROWS * LAND * DEPTH * 4
    shapes = (
        jax.ShapeDtypeStruct((ROWS, COLS), BF16),
        jax.ShapeDtypeStruct((BLOCK, COLS), F32),
    )
    return pl.pallas_call(
        body,
        out_shape=shapes,
        in_specs=[hbm] * 4,
        out_specs=(hbm, hbm),
        scratch_shapes=[
            vmem((2, ROWS, DEPTH), BF16),
            vmem((BLOCK, DEPTH), BF16),
            vmem((CHUNKS, BLOCK, PIECE), BF16),
            vmem((LAND, DEPTH), BF16),
            vmem((WCHUNKS, LAND, PIECE), BF16),
            vmem((ROWS, LAND), BF16),
            vmem((16, ROWS, PIECE), BF16),
            vmem((8, COLS, HALF), BF16),
            vmem((COLS, ROWS), F32),
            vmem((COLS, ROWS), BF16),
            vmem((3, COLS, HALF), BF16),
            vmem((4, COLS, 128), BF16),
            vmem((3, COLS, 128), BF16),
            vmem((4, 8, ROWS), F32),
            vmem((10, 8, COLS), F32),
            vmem((BLOCK, COLS), F32),
            pltpu.SemaphoreType.DMA((NSEND,)),
            pltpu.SemaphoreType.DMA((NRECV,)),
            pltpu.SemaphoreType.DMA((20,)),
            pltpu.SemaphoreType.REGULAR,
        ],
        compiler_params=pltpu.CompilerParams(
            collective_id=0, has_side_effects=True, vmem_limit_bytes=62 << 20
        ),
        cost_estimate=pl.CostEstimate(flops=flops, bytes_accessed=16 << 20, transcendentals=0),
        name="kmeans_step",
    )(descriptors, landmarks, whitening, centroids)


def solution(mesh):
    in_specs = (P("blk", None), P("blk", None), P("blk", "cent"), P("cent", None))
    out_specs = (P("blk", "cent"), P("blk", "cent"))
    return jax.shard_map(
        per_device, mesh=mesh, in_specs=in_specs, out_specs=out_specs, check_vma=False
    )
```
